512 devices in a mesh: seq: 128 (over z_lo, x, y), dp: 4 (over z_hi, core).
Axes of the slice: x: 4, y: 8, z: 8 (z_hi: 2, z_lo: 4; z = z_hi * 4 + z_lo), core: 2. Of those that a mesh axis runs over, the one named last changes fastest.
Arguments:
- byte_qkv: bfloat16 [4, 32768, 3072], P('dp', 'seq'), may hold values from -6 to 6
- patch_qkv: bfloat16 [4, 8192, 3072], P('dp', 'seq'), may hold values from -6 to 6
- patch_gain: float32 [3072], replicated, may hold values from 0.3 to 1.5
- out_grad: bfloat16 [4, 32768, 1024], P('dp', 'seq'), may hold values from -48 to 48
- patch_slot: int32 [4, 32768], P('dp', 'seq'), may hold values from 0 to 63, as said below
- lead: int32 [4, 128], P('dp', 'seq'), may hold values from 0 to 15, as said below
Outputs:
- byte_grad: bfloat16 [4, 32768, 3072], P('dp', 'seq')
- patch_grad: bfloat16 [4, 8192, 3072], P('dp', 'seq')
- gain_grad: float32 [3072], replicated
The draws below stay inside these ranges and needn't reach their ends.
Inputs may be any that keep to these rules, and one draw needn't show every extreme that they name: Patches are runs of 1 to 31 bytes of a stream. A patch is owned by the device that holds its first byte; each device numbers the patches starting on it 0, 1, 2 and so on in order, and patch_slot gives each byte the number of its patch on the owning device. Every device holds the first byte of at least one patch. lead[s, d] bytes at the start of device d's run of stream s belong to the last patch that starts on device d - 1; lead[s, 0] = 0.
All inputs are finite; a program needn't handle non-finite values.
Results may differ from the reference program's by a relative error of at most 0.011.
Values may be sent and summed in bfloat16 or wider, within the bound.
A program may use at most 128 MiB of HBM per device.

```python
import math
import jax
import jax.numpy as jnp
from jax import lax

HEADS = 8
HEAD_DIM = 128
WIN = 512
TOK_DEV = 256
P_CAP = 64
STREAMS = 4
SEQ_LEN = 32768
N_SEQ = 128


def patch_layout(key):
    folded = jax.random.fold_in(key, 11)
    k_level, k_wide, k_dense, k_offset = jax.random.split(folded, 4)
    level = jax.random.randint(k_level, (STREAMS, N_SEQ), 0, 3)
    wide_shard = 1 + jax.random.randint(k_wide, (STREAMS, 1), 0, N_SEQ - 1)
    dense_shard = (wide_shard + 1 + jax.random.randint(k_dense, (STREAMS, 1), 0, N_SEQ - 1)) % N_SEQ
    shard_ids = jnp.arange(N_SEQ, dtype=jnp.int32)[None, :]
    level = jnp.where(shard_ids == dense_shard, 0, level)
    level = jnp.where(shard_ids == wide_shard, 2, level)
    group_size = jnp.left_shift(jnp.full(level.shape, 4, jnp.int32), level)
    positions = jnp.arange(TOK_DEV, dtype=jnp.int32)[None, None, :]
    block_index = positions // group_size[:, :, None]
    offsets = jax.random.randint(k_offset, (STREAMS, N_SEQ, TOK_DEV // 4), 0, 16)
    chosen = jnp.take_along_axis(offsets, block_index, axis=2) % group_size[:, :, None]
    first_block = block_index == 0
    chosen = jnp.where(first_block & (shard_ids[:, :, None] == wide_shard[:, :, None]), 15, chosen)
    chosen = jnp.where(first_block & (shard_ids[:, :, None] == 0), 0, chosen)
    boundary = positions % group_size[:, :, None] == chosen
    counts = jnp.cumsum(boundary.astype(jnp.int32), axis=2)
    patches = TOK_DEV // group_size
    before = jnp.roll(patches, 1, axis=1)
    slot_ids = jnp.where(counts == 0, before[:, :, None] - 1, counts - 1)
    lead_counts = jnp.sum((counts == 0).astype(jnp.int32), axis=2)
    return (slot_ids.reshape(STREAMS, N_SEQ * TOK_DEV).astype(jnp.int32), lead_counts.astype(jnp.int32))


def draw_patch_slot(key, part):
    return patch_layout(key)[0]


def draw_lead(key, part):
    return patch_layout(key)[1]


def draw_byte_qkv(key, part):
    feature_count = HEADS * HEAD_DIM
    k_base = jax.random.fold_in(jax.random.fold_in(key, 23), 0)
    shape = (STREAMS, SEQ_LEN, 3 * feature_count)
    values = jnp.clip(jax.random.normal(k_base, shape, jnp.float32), -6.0, 6.0)
    return values.astype(jnp.bfloat16)


def block_levels(stream_key, extent, shards, least, high):
    gain = 1.0
    for position, blocks in shards:
        draws = jax.random.uniform(jax.random.fold_in(jax.random.fold_in(stream_key, 6), position), (blocks,), jnp.float32, least / len(shards), high / len(shards))
        gain = gain * jnp.repeat(jnp.exp(draws), extent[position] // blocks).reshape((-1,) + (1,) * (len(extent) - 1 - position))
    return gain


def scatter_about(stream_key, extent, width, bound, cuts=(), held_as=jnp.bfloat16):
    values = jax.random.normal(stream_key, extent, jnp.float32) * width
    if len(cuts) > 0:
        values = block_levels(stream_key, extent, cuts, -0.22, 0.18) * values
    return jnp.clip(values, min=-bound, max=bound).astype(held_as)


def setup_inputs(seed: int = 0) -> dict:
    arg_keys = jax.random.split(jax.random.key(seed), 7)
    byte_qkv = draw_byte_qkv(jax.random.fold_in(arg_keys[6], 71), 0)
    patch_qkv = scatter_about(arg_keys[1], (STREAMS, N_SEQ * P_CAP, 3 * HEADS * HEAD_DIM), 1.0, 6.0, ((0, 4), (1, 128)))
    patch_gain = jnp.clip(jnp.exp(jax.random.uniform(arg_keys[2], (3 * HEADS * HEAD_DIM,), jnp.float32, math.log(0.3), math.log(1.5))), 0.3, 1.5)
    out_grad = scatter_about(arg_keys[3], (STREAMS, SEQ_LEN, HEADS * HEAD_DIM), 8.0, 48.0, ((0, 4), (1, 128)))
    patch_slot = draw_patch_slot(jax.random.fold_in(arg_keys[6], 71), 0)
    lead = draw_lead(jax.random.fold_in(arg_keys[6], 71), 0)
    return dict(byte_qkv=byte_qkv, patch_qkv=patch_qkv, patch_gain=patch_gain, out_grad=out_grad, patch_slot=patch_slot, lead=lead)


def to_half(values):
    return lax.optimization_barrier(values.astype(jnp.bfloat16)).astype(jnp.float32)

def head_block(queries, keys, values, cotangent, query_pos, key_pos):
    inv_sqrt = 1.0 / math.sqrt(HEAD_DIM)
    scores = jnp.einsum('qhe,khe->hqk', queries, keys) * inv_sqrt
    in_window = (key_pos[None, :] <= query_pos[:, None]) & (key_pos[None, :] > query_pos[:, None] - WIN) & (key_pos[None, :] >= 0)
    scores = jnp.where(in_window[None], scores, -jnp.inf)
    row_max = lax.optimization_barrier(jnp.max(scores, axis=-1, keepdims=True))
    exponent = jnp.where(in_window[None], jnp.exp(scores - row_max), 0.0)
    probs = exponent / lax.optimization_barrier(jnp.sum(exponent, axis=-1, keepdims=True))
    probs_half = to_half(probs)
    value_grad = jnp.einsum('hqk,qhe->khe', probs_half, cotangent)
    prob_grad = jnp.einsum('qhe,khe->hqk', cotangent, values)
    row_delta = lax.optimization_barrier(jnp.sum(probs * prob_grad, axis=-1, keepdims=True))
    score_grad = to_half(probs * (prob_grad - row_delta))
    query_grad = jnp.einsum('hqk,khe->qhe', score_grad, keys) * inv_sqrt
    key_grad = jnp.einsum('hqk,qhe->khe', score_grad, queries) * inv_sqrt
    return (query_grad, key_grad, value_grad)

def stream_grads(hidden, cotangent):
    length = hidden.shape[0]
    hidden_f = hidden.astype(jnp.float32).reshape(length, 3, HEADS, HEAD_DIM)
    queries = hidden_f[:, 0]
    keys = hidden_f[:, 1]
    values = hidden_f[:, 2]
    cot_f = cotangent.astype(jnp.float32).reshape(length, HEADS, HEAD_DIM)
    padding = jnp.zeros((WIN, HEADS, HEAD_DIM), jnp.float32)
    keys_pad = jnp.concatenate([padding, keys], axis=0)
    values_pad = jnp.concatenate([padding, values], axis=0)

    def step(carry, block_index):
        key_acc, value_acc = carry
        first = (block_index * WIN).astype(jnp.int32)
        query_blk = lax.dynamic_slice_in_dim(queries, first, WIN, 0)
        cot_blk = lax.dynamic_slice_in_dim(cot_f, first, WIN, 0)
        key_blk = lax.dynamic_slice_in_dim(keys_pad, first, 2 * WIN, 0)
        value_blk = lax.dynamic_slice_in_dim(values_pad, first, 2 * WIN, 0)
        query_pos = first + jnp.arange(WIN, dtype=jnp.int32)
        key_pos = first - WIN + jnp.arange(2 * WIN, dtype=jnp.int32)
        query_grad, key_grad, value_grad = head_block(query_blk, key_blk, value_blk, cot_blk, query_pos, key_pos)
        key_acc = lax.dynamic_update_slice_in_dim(key_acc, lax.dynamic_slice_in_dim(key_acc, first, 2 * WIN, 0) + key_grad, first, 0)
        value_acc = lax.dynamic_update_slice_in_dim(value_acc, lax.dynamic_slice_in_dim(value_acc, first, 2 * WIN, 0) + value_grad, first, 0)
        return ((key_acc, value_acc), query_grad)
    start_acc = jnp.zeros((length + WIN, HEADS, HEAD_DIM), jnp.float32)
    (key_acc, value_acc), query_parts = lax.scan(step, (start_acc, start_acc), jnp.arange(length // WIN, dtype=jnp.int32))
    feature_count = HEADS * HEAD_DIM
    query_grad = query_parts.reshape(length, feature_count)
    key_grad = key_acc[WIN:].reshape(length, feature_count)
    value_grad = value_acc[WIN:].reshape(length, feature_count)
    return jnp.concatenate([query_grad, key_grad, value_grad], axis=1)

def reference(byte_qkv, patch_qkv, patch_gain, out_grad, patch_slot, lead):
    byte_pos = jnp.arange(SEQ_LEN, dtype=jnp.int32)
    shard_of = byte_pos // TOK_DEV
    local_pos = byte_pos - shard_of * TOK_DEV
    gain_total = jnp.zeros((3 * HEADS * HEAD_DIM,), jnp.float32)
    byte_out = []
    patch_out = []
    for stream in range(STREAMS):
        lead_here = lead[stream][shard_of]
        owner = jnp.where(local_pos >= lead_here, shard_of, shard_of - 1)
        slot_rows = (owner * P_CAP + patch_slot[stream]).astype(jnp.int32)
        patch_rows = patch_qkv[stream][slot_rows]
        hidden = (patch_gain * patch_rows.astype(jnp.float32) + byte_qkv[stream].astype(jnp.float32)).astype(jnp.bfloat16)
        hidden_grad = stream_grads(hidden, out_grad[stream])
        byte_out.append(hidden_grad.astype(jnp.bfloat16))
        slot_sums = jax.ops.segment_sum(hidden_grad, slot_rows, num_segments=N_SEQ * P_CAP)
        patch_out.append((patch_gain * slot_sums).astype(jnp.bfloat16))
        gain_total = gain_total + lax.optimization_barrier(jnp.sum(hidden_grad * patch_rows.astype(jnp.float32), axis=0))
    return (jnp.stack(byte_out), jnp.stack(patch_out), gain_total / TOK_DEV)
```

```python
import functools
import math

import jax
import jax.numpy as jnp
from jax import lax
from jax.experimental import pallas as pl
from jax.experimental.pallas import tpu as pltpu
from jax.sharding import PartitionSpec as P

HEADS = 8
HD = 128
ROWS = 256
CAP = 64
N_SEQ = 128
MESH = pl.DeviceIdType.MESH
BF = jnp.bfloat16
F32 = jnp.float32

NEG = -1e9
SCALE = 1.0 / math.sqrt(HD)
SCALE2 = SCALE / math.log(2.0)
AHEAD = 3
LAG2 = 3
LAG3 = 5
LAG4 = 6
SLOTS = LAG2 + 1

K_Q, K_DO, K_KV, K_SA, K_SB, K_DKV, K_DQ, K_LS = range(8)


def nt(a, b):
    return lax.dot_general(a, b, (((1,), (1,)), ((), ())), preferred_element_type=F32)


def nn(a, b):
    return lax.dot_general(a, b, (((1,), (0,)), ((), ())), preferred_element_type=F32)


def tn(a, b):
    return lax.dot_general(a, b, (((0,), (0,)), ((), ())), preferred_element_type=F32)


def cols(block):
    return pl.ds(pl.multiple_of(block * HD, HD), HD)


def peer_groups(me, dp):
    y = lax.rem(me, 8)
    x = lax.rem(me // 8, 4)
    z_lo = me // 32
    z_hi = dp // 2
    core = lax.rem(dp, 2)
    along_z, along_xc, along_y = [], [], []
    for k in range(1, 8):
        z = lax.rem(z_hi * 4 + z_lo + k, 8)
        along_z.append(((lax.rem(z, 4) * 4 + x) * 8 + y, (z // 4) * 2 + core))
        p = lax.rem(x * 2 + core + k, 8)
        along_xc.append(((z_lo * 4 + p // 2) * 8 + y, z_hi * 2 + lax.rem(p, 2)))
        along_y.append(((z_lo * 4 + x) * 8 + lax.rem(y + k, 8), dp))
    return along_z, along_xc, along_y


def kernel(
    byte_ref,
    patch_ref,
    gain_ref,
    cot_ref,
    slot_ref,
    lead_ref,
    bg_ref,
    pg_ref,
    gg_ref,
    byte_v,
    tab_v,
    oh,
    mem,
    qdo_own,
    kv_own,
    qdo_nxt,
    kv_prv,
    dq_loc,
    dkv_loc,
    dq_snd,
    dkv_snd,
    dq_rcv,
    dkv_rcv,
    pbuf,
    dpbuf,
    sa_own,
    sa_nxt,
    sb_own,
    sb_rcv,
    prev_snd,
    prev_rcv,
    ls_snd,
    ls_rcv,
    last_col,
    ssum,
    out_b,
    out_p,
    g_acc,
    g_rcv,
    in_sem,
    do_sem,
    s_sem,
    r_sem,
    prev_sem,
    ob_sem,
    op_sem,
    gs_sem,
    gr_sem,
):
    me = lax.axis_index("seq")
    dp = lax.axis_index("dp")
    has_left = me > 0
    has_right = me < N_SEQ - 1
    left = (me - 1, dp)
    right = (me + 1, dp)
    groups = peer_groups(me, dp)

    barrier = pltpu.get_barrier_semaphore()

    @pl.when(has_left)
    def _():
        pl.semaphore_signal(barrier, inc=1, device_id=left, device_id_type=MESH)

    @pl.when(has_right)
    def _():
        pl.semaphore_signal(barrier, inc=1, device_id=right, device_id_type=MESH)

    for group in groups:
        for peer in group:
            pl.semaphore_signal(barrier, inc=1, device_id=peer, device_id_type=MESH)

    load_tab = pltpu.make_async_copy(patch_ref.at[0], tab_v.at[pl.ds(0, CAP)], in_sem.at[0])
    load_tab.start()
    load_byte = pltpu.make_async_copy(byte_ref.at[0], byte_v, in_sem.at[1])
    load_byte.start()

    def load_do(h):
        return pltpu.make_async_copy(cot_ref.at[0, :, cols(h)], qdo_own.at[h, 1], do_sem.at[h])

    for h in range(HEADS):
        load_do(h).start()

    lead = lead_ref[0, 0]
    slots = slot_ref[...]
    row_i = lax.broadcasted_iota(jnp.int32, (HD, ROWS), 0)
    lane_i = lax.broadcasted_iota(jnp.int32, (HD, ROWS), 1)
    pick = jnp.where(row_i == slots, 1.0, 0.0)
    oh[...] = jnp.transpose(pick).astype(BF)
    mem[...] = jnp.where(lane_i < lead, jnp.where(row_i == CAP, 1.0, 0.0), pick)[:80].astype(BF)
    last_col[...] = jnp.broadcast_to(pick[:CAP, ROWS - 1 : ROWS], (CAP, HD))
    tab_v[CAP:] = jnp.zeros((HD - CAP, 3 * HEADS * HD), BF)

    @pl.when(jnp.logical_not(has_left))
    def _():
        kv_prv[...] = jnp.zeros_like(kv_prv)
        dq_rcv[...] = jnp.zeros_like(dq_rcv)
        prev_rcv[...] = jnp.zeros_like(prev_rcv)
        sb_rcv[...] = jnp.full(sb_rcv.shape, NEG, F32)

    @pl.when(jnp.logical_not(has_right))
    def _():
        qdo_nxt[...] = jnp.zeros_like(qdo_nxt)
        dkv_rcv[...] = jnp.zeros_like(dkv_rcv)
        ls_rcv[...] = jnp.zeros_like(ls_rcv)
        sa_nxt[...] = jnp.ones_like(sa_nxt)

    load_tab.wait()
    load_byte.wait()

    def hidden_dst(part, h):
        return qdo_own.at[h, 0] if part == 0 else kv_own.at[h, part - 1]

    def make_hidden(h, carry):
        for part in range(3):
            cb = part * HEADS + h
            rows = nn(oh[...], tab_v[:, cols(cb)])
            prev_snd[cb] = rows[ROWS - 1 : ROWS]
            hidden = gain_ref[:, cols(cb)] * rows + byte_v[:, cols(cb)].astype(F32)
            hidden_dst(part, h)[...] = hidden.astype(BF)
        return carry

    lax.fori_loop(0, HEADS, make_hidden, 0)
    for h in range(HEADS):
        load_do(h).wait()

    neighbours = has_left.astype(jnp.int32) + has_right.astype(jnp.int32)
    pl.semaphore_wait(barrier, neighbours + 21)

    def remote(kind, h, src, dst, to):
        return pltpu.make_async_remote_copy(
            src_ref=src,
            dst_ref=dst,
            send_sem=s_sem.at[kind, h],
            recv_sem=r_sem.at[kind, h],
            device_id=to,
            device_id_type=MESH,
        )

    def c_q(h):
        return remote(K_Q, h, qdo_own.at[h, 0], qdo_nxt.at[h, 0], left)

    def c_do(h):
        return remote(K_DO, h, qdo_own.at[h, 1], qdo_nxt.at[h, 1], left)

    def c_kv(h):
        return remote(K_KV, h, kv_own.at[h], kv_prv.at[h], right)

    def c_sa(h):
        return remote(K_SA, h, sa_own.at[h], sa_nxt.at[h], left)

    def c_sb(h):
        return remote(K_SB, h, sb_own.at[h], sb_rcv.at[h], right)

    def c_dkv(h):
        return remote(K_DKV, h, dkv_snd.at[h], dkv_rcv.at[h], left)

    def c_dq(h):
        return remote(K_DQ, h, dq_snd.at[h], dq_rcv.at[h], right)

    def c_ls(h):
        return remote(K_LS, h, ls_snd.at[h], ls_rcv.at[h], left)

    c_prev = pltpu.make_async_remote_copy(
        src_ref=prev_snd,
        dst_ref=prev_rcv,
        send_sem=prev_sem.at[0],
        recv_sem=prev_sem.at[1],
        device_id=right,
        device_id_type=MESH,
    )

    @pl.when(has_right)
    def _():
        c_prev.start()

    @pl.when(has_left)
    def _():
        for h in range(AHEAD):
            c_do(h).start()
        c_prev.wait_recv()

    lead_rows = lax.broadcasted_iota(jnp.int32, (16, HD), 0) < lead

    def fix_hidden(h, carry):
        for part in range(3):
            cb = part * HEADS + h
            dst = hidden_dst(part, h)
            fixed = gain_ref[:, cols(cb)] * prev_rcv[cb] + byte_v[:16, cols(cb)].astype(F32)
            dst[:16] = jnp.where(lead_rows, fixed, dst[:16].astype(F32)).astype(BF)
        return carry

    lax.fori_loop(0, HEADS, fix_hidden, 0)

    def send_inputs(h, with_do=True):
        @pl.when(has_left)
        def _():
            c_q(h).start()
            if with_do:
                c_do(h).start()

        @pl.when(has_right)
        def _():
            c_kv(h).start()

    for h in range(AHEAD):
        send_inputs(h, False)

    def phase1(h):
        slot = lax.rem(h, SLOTS)

        @pl.when(has_left)
        def _():
            c_kv(h).wait_recv()

        @pl.when(has_right)
        def _():
            c_q(h).wait_recv()
            c_do(h).wait_recv()

        key_i = lax.broadcasted_iota(jnp.int32, (ROWS, ROWS), 0)
        query_i = lax.broadcasted_iota(jnp.int32, (ROWS, ROWS), 1)
        bias_p = jnp.where(has_left, 0.0, NEG)
        bias_b = jnp.where(jnp.logical_and(has_left, has_right), 0.0, NEG)
        k_c, k_p = kv_own[h, 0], kv_prv[h, 0]
        q_o, q_n = qdo_own[h, 0], qdo_nxt[h, 0]
        s_c = jnp.where(key_i <= query_i, nt(k_c, q_o) * SCALE2, NEG)
        s_p = nt(k_p, q_o) * SCALE2 + bias_p
        m_a = jnp.maximum(
            jnp.max(s_c, axis=0, keepdims=True), jnp.max(s_p, axis=0, keepdims=True)
        )
        p_c = jnp.exp2(s_c - m_a)
        p_p = jnp.exp2(s_p - m_a)
        l_a = jnp.sum(p_c, axis=0, keepdims=True) + jnp.sum(p_p, axis=0, keepdims=True)
        dp_c = nt(kv_own[h, 1], qdo_own[h, 1])
        dp_p = nt(kv_prv[h, 1], qdo_own[h, 1])
        d_a = jnp.sum(p_c * dp_c, axis=0, keepdims=True) + jnp.sum(
            p_p * dp_p, axis=0, keepdims=True
        )
        pbuf[slot, 0] = p_c
        pbuf[slot, 1] = p_p
        dpbuf[slot, 0] = dp_c
        dpbuf[slot, 1] = dp_p
        sa_own[h, 0:1] = m_a
        sa_own[h, 1:2] = l_a
        sa_own[h, 2:3] = d_a
        sa_own[h, 3:4] = d_a

        @pl.when(has_left)
        def _():
            c_sa(h).start()

        s_b = jnp.where(key_i > query_i, nt(k_p, q_n) * SCALE2 + bias_b, NEG)
        m_b = jnp.max(s_b, axis=0, keepdims=True)
        p_b = jnp.exp2(s_b - m_b)
        l_b = jnp.sum(p_b, axis=0, keepdims=True)
        dp_b = nt(kv_prv[h, 1], qdo_nxt[h, 1])
        d_b = jnp.sum(p_b * dp_b, axis=0, keepdims=True)
        pbuf[slot, 2] = p_b
        dpbuf[slot, 2] = dp_b
        sb_own[h, 0:1] = m_b
        sb_own[h, 1:2] = l_b
        sb_own[h, 2:3] = d_b
        sb_own[h, 3:4] = d_b

        @pl.when(has_right)
        def _():
            c_sb(h).start()

    def combine(a, b):
        m_a, m_b = a[0:1], b[0:1]
        m = jnp.maximum(m_a, m_b)
        e_a = jnp.exp2(m_a - m)
        e_b = jnp.exp2(m_b - m)
        inv = 1.0 / (a[1:2] * e_a + b[1:2] * e_b)
        w_a = e_a * inv
        w_b = e_b * inv
        return w_a, w_b, a[2:3] * w_a + b[2:3] * w_b

    def phase2(h):
        slot = lax.rem(h, SLOTS)

        @pl.when(has_left)
        def _():
            c_sb(h).wait_recv()

        @pl.when(has_right)
        def _():
            c_sa(h).wait_recv()

        w_o, _, delta_o = combine(sa_own[h], sb_rcv[h])
        _, w_n, delta_n = combine(sa_nxt[h], sb_own[h])
        k_c, k_p = kv_own[h, 0], kv_prv[h, 0]
        q_o, q_n = qdo_own[h, 0], qdo_nxt[h, 0]
        do_o, do_n = qdo_own[h, 1], qdo_nxt[h, 1]
        p_b = pbuf[slot, 2] * w_n
        ds_b = (p_b * (dpbuf[slot, 2] - delta_n)).astype(BF)
        p_p = pbuf[slot, 1] * w_o
        ds_p = (p_p * (dpbuf[slot, 1] - delta_o)).astype(BF)
        dkv_snd[h, 0] = ((nn(ds_p, q_o) + nn(ds_b, q_n)) * SCALE).astype(BF)
        dkv_snd[h, 1] = (nn(p_p.astype(BF), do_o) + nn(p_b.astype(BF), do_n)).astype(BF)

        @pl.when(has_left)
        def _():
            c_dkv(h).start()

        dq_snd[h] = (tn(ds_b, k_p) * SCALE).astype(BF)

        @pl.when(has_right)
        def _():
            c_dq(h).start()

        p_c = pbuf[slot, 0] * w_o
        ds_c = (p_c * (dpbuf[slot, 0] - delta_o)).astype(BF)
        dkv_loc[h, 0] = nn(ds_c, q_o) * SCALE
        dkv_loc[h, 1] = nn(p_c.astype(BF), do_o)
        dq_loc[h] = (tn(ds_c, k_c) + tn(ds_p, k_p)) * SCALE

    def out_byte(part, h):
        cb = part * HEADS + h
        return pltpu.make_async_copy(
            out_b.at[h, part], bg_ref.at[0, :, cols(cb)], ob_sem.at[h, part]
        )

    def out_patch(part, h):
        cb = part * HEADS + h
        return pltpu.make_async_copy(
            out_p.at[h, part], pg_ref.at[0, :, cols(cb)], op_sem.at[h, part]
        )

    def results(h):
        @pl.when(has_left)
        def _():
            c_dq(h).wait_recv()

        @pl.when(has_right)
        def _():
            c_dkv(h).wait_recv()

        for part in range(3):
            cb = part * HEADS + h
            if part == 0:
                grad = dq_loc[h] + dq_rcv[h].astype(F32)
            else:
                grad = dkv_loc[h, part - 1] + dkv_rcv[h, part - 1].astype(F32)
            high = grad.astype(BF)
            out_b[h, part] = high
            low = (grad - high.astype(F32)).astype(BF)
            sums = nn(mem[...], high) + nn(mem[...], low)
            ssum[h, part] = sums[:CAP]
            lead_sum = sums[CAP : CAP + 1]
            ls_snd[h, part : part + 1] = lead_sum
            if part == 0:
                ls_snd[h, 3:4] = lead_sum
            table = tab_v[:CAP, cols(cb)].astype(F32)
            g_acc[0, cb] = (
                jnp.sum(sums[:CAP] * table, axis=0, keepdims=True) + lead_sum * prev_rcv[cb]
            )
            out_byte(part, h).start()

        @pl.when(has_left)
        def _():
            c_ls(h).start()

    def patch_results(h):
        @pl.when(has_right)
        def _():
            c_ls(h).wait_recv()

        for part in range(3):
            cb = part * HEADS + h
            total = ssum[h, part] + last_col[...] * ls_rcv[h, part : part + 1]
            out_p[h, part] = (total * gain_ref[:, cols(cb)]).astype(BF)
            out_patch(part, h).start()

    def step(s, carry):
        @pl.when(s < HEADS)
        def _():
            phase1(s)

        @pl.when(s < HEADS - AHEAD)
        def _():
            send_inputs(s + AHEAD)

        @pl.when(jnp.logical_and(s >= LAG2, s < HEADS + LAG2))
        def _():
            phase2(s - LAG2)

        @pl.when(jnp.logical_and(s >= LAG3, s < HEADS + LAG3))
        def _():
            results(s - LAG3)

        @pl.when(jnp.logical_and(s >= LAG4, s < HEADS + LAG4))
        def _():
            patch_results(s - LAG4)

        return carry

    lax.fori_loop(0, HEADS + LAG4, step, 0)

    for t, group in enumerate(groups):
        copies = []
        for k, peer in enumerate(group):
            copy = pltpu.make_async_remote_copy(
                src_ref=g_acc.at[t],
                dst_ref=g_rcv.at[t, k],
                send_sem=gs_sem.at[t, k],
                recv_sem=gr_sem.at[t, k],
                device_id=peer,
                device_id_type=MESH,
            )
            copy.start()
            copies.append(copy)
        for copy in copies:
            copy.wait_recv()
        total = g_acc[t]
        for k in range(7):
            total = total + g_rcv[t, k]
        if t < 2:
            g_acc[t + 1] = total
        else:
            gg_ref[...] = total / ROWS
        for copy in copies:
            copy.wait_send()

    def drain(h, carry):
        @pl.when(has_left)
        def _():
            for copy in (c_q(h), c_do(h), c_sa(h), c_dkv(h), c_ls(h)):
                copy.wait_send()

        @pl.when(has_right)
        def _():
            for copy in (c_kv(h), c_sb(h), c_dq(h)):
                copy.wait_send()

        for part in range(3):
            out_byte(part, h).wait()
            out_patch(part, h).wait()
        return carry

    lax.fori_loop(0, HEADS, drain, 0)

    @pl.when(has_right)
    def _():
        c_prev.wait_send()


def local(byte_qkv, patch_qkv, patch_gain, out_grad, patch_slot, lead):
    width = 3 * HEADS * HD
    any_spec = pl.BlockSpec(memory_space=pl.ANY)
    vmem = pl.BlockSpec(memory_space=pltpu.VMEM)
    smem = pl.BlockSpec(memory_space=pltpu.SMEM)
    V = pltpu.VMEM
    byte_grad, patch_grad, gain_grad = pl.pallas_call(
        kernel,
        out_shape=(
            jax.ShapeDtypeStruct((1, ROWS, width), BF),
            jax.ShapeDtypeStruct((1, CAP, width), BF),
            jax.ShapeDtypeStruct((3 * HEADS, 1, HD), F32),
        ),
        in_specs=[any_spec, any_spec, vmem, any_spec, vmem, smem],
        out_specs=(any_spec, any_spec, vmem),
        scratch_shapes=[
            V((ROWS, width), BF),
            V((HD, width), BF),
            V((ROWS, HD), BF),
            V((80, ROWS), BF),
            V((HEADS, 2, ROWS, HD), BF),
            V((HEADS, 2, ROWS, HD), BF),
            V((HEADS, 2, ROWS, HD), BF),
            V((HEADS, 2, ROWS, HD), BF),
            V((HEADS, ROWS, HD), F32),
            V((HEADS, 2, ROWS, HD), F32),
            V((HEADS, ROWS, HD), BF),
            V((HEADS, 2, ROWS, HD), BF),
            V((HEADS, ROWS, HD), BF),
            V((HEADS, 2, ROWS, HD), BF),
            V((SLOTS, 3, ROWS, ROWS), F32),
            V((SLOTS, 3, ROWS, ROWS), F32),
            V((HEADS, 4, ROWS), F32),
            V((HEADS, 4, ROWS), F32),
            V((HEADS, 4, ROWS), F32),
            V((HEADS, 4, ROWS), F32),
            V((3 * HEADS, 1, HD), F32),
            V((3 * HEADS, 1, HD), F32),
            V((HEADS, 4, HD), F32),
            V((HEADS, 4, HD), F32),
            V((CAP, HD), F32),
            V((HEADS, 3, CAP, HD), F32),
            V((HEADS, 3, ROWS, HD), BF),
            V((HEADS, 3, CAP, HD), BF),
            V((3, 3 * HEADS, 1, HD), F32),
            V((3, 7, 3 * HEADS, 1, HD), F32),
            pltpu.SemaphoreType.DMA((2,)),
            pltpu.SemaphoreType.DMA((HEADS,)),
            pltpu.SemaphoreType.DMA((8, HEADS)),
            pltpu.SemaphoreType.DMA((8, HEADS)),
            pltpu.SemaphoreType.DMA((2,)),
            pltpu.SemaphoreType.DMA((HEADS, 3)),
            pltpu.SemaphoreType.DMA((HEADS, 3)),
            pltpu.SemaphoreType.DMA((3, 7)),
            pltpu.SemaphoreType.DMA((3, 7)),
        ],
        compiler_params=pltpu.CompilerParams(
            collective_id=0, has_side_effects=True, vmem_limit_bytes=48 * 2**20
        ),
    )(byte_qkv, patch_qkv, patch_gain.reshape(1, width), out_grad, patch_slot, lead)
    return byte_grad, patch_grad, gain_grad.reshape(width)


def solution(mesh):
    placed = (
        P("dp", "seq", None),
        P("dp", "seq", None),
        P(),
        P("dp", "seq", None),
        P("dp", "seq"),
        P("dp", "seq"),
    )
    return jax.shard_map(
        local,
        mesh=mesh,
        in_specs=placed,
        out_specs=(P("dp", "seq", None), P("dp", "seq", None), P()),
        check_vma=False,
    )
```

```python
import functools
import math

import jax
import jax.numpy as jnp
from jax import lax
from jax.experimental import pallas as pl
from jax.experimental.pallas import tpu as pltpu
from jax.sharding import PartitionSpec as P

HEADS = 8
HD = 128
ROWS = 256
CAP = 64
N_SEQ = 128
MESH = pl.DeviceIdType.MESH
BF = jnp.bfloat16
F32 = jnp.float32

NEG = -1e9
SCALE = 1.0 / math.sqrt(HD)
SCALE2 = SCALE / math.log(2.0)
AHEAD = 3
LAG2 = 3
EXT = 80
SLOTS = LAG2 + 1
FLIGHT = 3
HOLD = 6
FIRST = 7

K_Q, K_DO, K_KV, K_SA, K_SB, K_DKV, K_DQ, K_TQ, K_TX = range(9)
O_PREV, O_EL, O_ER, O_LP, O_LS = range(5)


def nt(a, b):
    return lax.dot_general(a, b, (((1,), (1,)), ((), ())), preferred_element_type=F32)


def nn(a, b):
    return lax.dot_general(a, b, (((1,), (0,)), ((), ())), preferred_element_type=F32)


def tn(a, b):
    return lax.dot_general(a, b, (((0,), (0,)), ((), ())), preferred_element_type=F32)


def cols(block):
    return pl.ds(pl.multiple_of(block * HD, HD), HD)


def peer_groups(me, dp):
    y = lax.rem(me, 8)
    x = lax.rem(me // 8, 4)
    z_lo = me // 32
    z_hi = dp // 2
    core = lax.rem(dp, 2)
    along_z, along_xc, along_y = [], [], []
    for k in range(1, 8):
        z = lax.rem(z_hi * 4 + z_lo + k, 8)
        along_z.append(((lax.rem(z, 4) * 4 + x) * 8 + y, (z // 4) * 2 + core))
        p = lax.rem(x * 2 + core + k, 8)
        along_xc.append(((z_lo * 4 + p // 2) * 8 + y, z_hi * 2 + lax.rem(p, 2)))
        along_y.append(((z_lo * 4 + x) * 8 + lax.rem(y + k, 8), dp))
    return along_y, along_z, along_xc


def kernel(
    byte_ref,
    patch_ref,
    gain_ref,
    cot_ref,
    slot_ref,
    lead_ref,
    bg_ref,
    pg_ref,
    gg_ref,
    byte_v,
    tabq,
    tabx,
    tabq_rcv,
    tabx_rcv,
    oh,
    mem,
    mem_l,
    mem_r,
    effs,
    effs_l,
    effs_r,
    qdo_own,
    kv_own,
    qdo_nxt,
    kv_prv,
    dq_loc,
    dkv_loc,
    dq_snd,
    dkv_snd,
    dq_rcv,
    dkv_rcv,
    pbuf,
    dpbuf,
    sa_own,
    sa_nxt,
    sb_own,
    sb_rcv,
    prev_snd,
    prev_rcv,
    lp_snd,
    lp_rcv,
    ls_snd,
    ls_rcv,
    from_q,
    last_col,
    ssum,
    out_b,
    out_p,
    g_acc,
    g_rcv,
    in_sem,
    do_sem,
    tab_sem,
    s_sem,
    r_sem,
    one_s,
    one_r,
    hi_sem,
    ob_sem,
    op_sem,
    gs_sem,
    gr_sem,
):
    me = lax.axis_index("seq")
    dp = lax.axis_index("dp")
    has_left = me > 0
    has_right = me < N_SEQ - 1
    left = (me - 1, dp)
    right = (me + 1, dp)
    groups = peer_groups(me, dp)

    barrier = pltpu.get_barrier_semaphore()

    @pl.when(has_left)
    def _():
        pl.semaphore_signal(barrier, inc=1, device_id=left, device_id_type=MESH)

    @pl.when(has_right)
    def _():
        pl.semaphore_signal(barrier, inc=1, device_id=right, device_id_type=MESH)

    z_lo = me // 32
    z_hi = dp // 2
    place = lax.rem(me, 32)
    other_half = [(k * 32 + place, (1 - z_hi) * 2 + lax.rem(dp, 2)) for k in range(4)]
    same_half = [(lax.rem(z_lo + k, 4) * 32 + place, dp) for k in range(1, 4)]
    for peer in groups[0] + groups[2] + same_half:
        pl.semaphore_signal(barrier, inc=1, device_id=peer, device_id_type=MESH)

    @pl.when(z_hi == 0)
    def _():
        for peer in other_half:
            pl.semaphore_signal(barrier, inc=1, device_id=peer, device_id_type=MESH)

    def load_tables(h):
        return [
            pltpu.make_async_copy(
                patch_ref.at[0, :, cols(h)], tabq.at[h], tab_sem.at[h, 0]
            )
        ] + [
            pltpu.make_async_copy(
                patch_ref.at[0, :, cols((part + 1) * HEADS + h)],
                tabx.at[h, part, pl.ds(0, CAP)],
                tab_sem.at[h, part + 1],
            )
            for part in range(2)
        ]

    for h in range(HEADS):
        for load in load_tables(h):
            load.start()
    load_byte = pltpu.make_async_copy(byte_ref.at[0], byte_v, in_sem.at[0])
    load_byte.start()

    def load_do(h):
        return pltpu.make_async_copy(cot_ref.at[0, :, cols(h)], qdo_own.at[h, 1], do_sem.at[h])

    for h in range(HEADS):
        load_do(h).start()

    lead = lead_ref[0, 0]
    slots = slot_ref[...]
    lane_i = lax.broadcasted_iota(jnp.int32, (1, ROWS), 1)
    effs[...] = jnp.where(lane_i < lead, CAP, slots).astype(F32)

    def members(eff):
        row_i = lax.broadcasted_iota(jnp.int32, (EXT, ROWS), 0).astype(F32)
        return jnp.where(row_i == eff, 1.0, 0.0).astype(BF)

    mem[...] = members(effs[...])
    slot_i = lax.broadcasted_iota(jnp.int32, (HD, ROWS), 0)
    pick = jnp.where(slot_i == slots, 1.0, 0.0)
    oh[...] = jnp.transpose(pick)[:, :CAP].astype(BF)
    last_col[...] = jnp.broadcast_to(pick[:CAP, ROWS - 1 : ROWS], (CAP, HD))

    @pl.when(jnp.logical_not(has_left))
    def _():
        kv_prv[...] = jnp.zeros_like(kv_prv)
        tabx_rcv[...] = jnp.zeros_like(tabx_rcv)
        effs_l[...] = jnp.zeros_like(effs_l)
        dq_rcv[...] = jnp.zeros_like(dq_rcv)
        prev_rcv[...] = jnp.zeros_like(prev_rcv)
        sb_rcv[...] = jnp.full(sb_rcv.shape, NEG, F32)

    @pl.when(jnp.logical_not(has_right))
    def _():
        qdo_nxt[...] = jnp.zeros_like(qdo_nxt)
        dkv_rcv[...] = jnp.zeros_like(dkv_rcv)
        ls_rcv[...] = jnp.zeros_like(ls_rcv)
        lp_rcv[...] = jnp.zeros_like(lp_rcv)
        tabq_rcv[...] = jnp.zeros_like(tabq_rcv)
        effs_r[...] = jnp.zeros_like(effs_r)
        sa_nxt[...] = jnp.ones_like(sa_nxt)

    for h in range(HEADS):
        for load in load_tables(h):
            load.wait()
    load_byte.wait()

    def hidden_dst(part, h):
        return qdo_own.at[h, 0] if part == 0 else kv_own.at[h, part - 1]

    def make_hidden(h, carry):
        for part in range(3):
            cb = part * HEADS + h
            rows = nn(oh[...], tabq[h] if part == 0 else tabx[h, part - 1, :CAP])
            prev_snd[cb] = rows[ROWS - 1 : ROWS]
            hidden = gain_ref[:, cols(cb)] * rows + byte_v[:, cols(cb)].astype(F32)
            hidden_dst(part, h)[...] = hidden.astype(BF)
        return carry

    lax.fori_loop(0, HEADS, make_hidden, 0)
    for h in range(HEADS):
        load_do(h).wait()

    neighbours = has_left.astype(jnp.int32) + has_right.astype(jnp.int32)
    pl.semaphore_wait(barrier, neighbours + 17 + 4 * z_hi)

    @pl.when(z_hi == 1)
    def _():
        for peer in other_half:
            pl.semaphore_signal(hi_sem, inc=1, device_id=peer, device_id_type=MESH)


    def remote(kind, h, src, dst, to):
        return pltpu.make_async_remote_copy(
            src_ref=src,
            dst_ref=dst,
            send_sem=s_sem.at[kind, h],
            recv_sem=r_sem.at[kind, h],
            device_id=to,
            device_id_type=MESH,
        )

    def c_q(h):
        return remote(K_Q, h, qdo_own.at[h, 0], qdo_nxt.at[h, 0], left)

    def c_do(h):
        return remote(K_DO, h, qdo_own.at[h, 1], qdo_nxt.at[h, 1], left)

    def c_kv(h):
        return remote(K_KV, h, kv_own.at[h], kv_prv.at[h], right)

    def c_sa(h):
        return remote(K_SA, h, sa_own.at[h], sa_nxt.at[h], left)

    def c_sb(h):
        return remote(K_SB, h, sb_own.at[h], sb_rcv.at[h], right)

    def c_dkv(h):
        return remote(K_DKV, h, dkv_snd.at[h], dkv_rcv.at[h], left)

    def c_dq(h):
        return remote(K_DQ, h, dq_snd.at[h], dq_rcv.at[h], right)

    def c_tq(h):
        return remote(K_TQ, h, tabq.at[h], tabq_rcv.at[h], left)

    def c_tx(h):
        return remote(K_TX, h, tabx.at[h], tabx_rcv.at[h], right)

    def once(kind, src, dst, to):
        return pltpu.make_async_remote_copy(
            src_ref=src,
            dst_ref=dst,
            send_sem=one_s.at[kind],
            recv_sem=one_r.at[kind],
            device_id=to,
            device_id_type=MESH,
        )

    c_prev = once(O_PREV, prev_snd, prev_rcv, right)
    c_el = once(O_EL, effs, effs_r, left)
    c_er = once(O_ER, effs, effs_l, right)
    c_lp = once(O_LP, lp_snd, lp_rcv, left)
    c_ls = once(O_LS, ls_snd, ls_rcv, left)

    @pl.when(has_right)
    def _():
        c_prev.start()
        c_er.start()

    @pl.when(has_left)
    def _():
        c_el.start()
        for h in range(AHEAD):
            c_do(h).start()
        c_prev.wait_recv()

    lead_rows = lax.broadcasted_iota(jnp.int32, (16, HD), 0) < lead

    first_row = lax.broadcasted_iota(jnp.int32, (EXT - CAP, HD), 0) == 0

    def fix_hidden(h, carry):
        for part in range(3):
            cb = part * HEADS + h
            if part > 0:
                tabx[h, part - 1, CAP:] = jnp.where(first_row, prev_rcv[cb], 0.0).astype(BF)
            dst = hidden_dst(part, h)
            fixed = gain_ref[:, cols(cb)] * prev_rcv[cb] + byte_v[:16, cols(cb)].astype(F32)
            dst[:16] = jnp.where(lead_rows, fixed, dst[:16].astype(F32)).astype(BF)
        return carry

    lax.fori_loop(0, HEADS, fix_hidden, 0)

    def send_inputs(h, with_do=True):
        @pl.when(has_left)
        def _():
            c_q(h).start()
            if with_do:
                c_do(h).start()

        @pl.when(has_right)
        def _():
            c_kv(h).start()

    for h in range(AHEAD):
        send_inputs(h, False)

    @pl.when(has_left)
    def _():
        c_er.wait_recv()

    @pl.when(has_right)
    def _():
        c_el.wait_recv()

    mem_l[...] = members(effs_l[...])
    mem_r[...] = members(effs_r[...])

    def phase1(h):
        slot = lax.rem(h, SLOTS)

        @pl.when(has_left)
        def _():
            c_kv(h).wait_recv()

        @pl.when(has_right)
        def _():
            c_q(h).wait_recv()
            c_do(h).wait_recv()

        key_i = lax.broadcasted_iota(jnp.int32, (ROWS, ROWS), 0)
        query_i = lax.broadcasted_iota(jnp.int32, (ROWS, ROWS), 1)
        bias_p = jnp.where(has_left, 0.0, NEG)
        bias_b = jnp.where(jnp.logical_and(has_left, has_right), 0.0, NEG)
        k_c, k_p = kv_own[h, 0], kv_prv[h, 0]
        q_o, q_n = qdo_own[h, 0], qdo_nxt[h, 0]
        s_c = jnp.where(key_i <= query_i, nt(k_c, q_o) * SCALE2, NEG)
        s_p = nt(k_p, q_o) * SCALE2 + bias_p
        m_a = jnp.maximum(
            jnp.max(s_c, axis=0, keepdims=True), jnp.max(s_p, axis=0, keepdims=True)
        )
        p_c = jnp.exp2(s_c - m_a)
        p_p = jnp.exp2(s_p - m_a)
        l_a = jnp.sum(p_c, axis=0, keepdims=True) + jnp.sum(p_p, axis=0, keepdims=True)
        dp_c = nt(kv_own[h, 1], qdo_own[h, 1])
        dp_p = nt(kv_prv[h, 1], qdo_own[h, 1])
        d_a = jnp.sum(p_c * dp_c, axis=0, keepdims=True) + jnp.sum(
            p_p * dp_p, axis=0, keepdims=True
        )
        pbuf[slot, 0] = p_c
        pbuf[slot, 1] = p_p
        dpbuf[slot, 0] = dp_c
        dpbuf[slot, 1] = dp_p
        sa_own[h, 0:1] = m_a
        sa_own[h, 1:2] = l_a
        sa_own[h, 2:3] = d_a
        sa_own[h, 3:4] = d_a

        @pl.when(has_left)
        def _():
            c_sa(h).start()

        s_b = jnp.where(key_i > query_i, nt(k_p, q_n) * SCALE2 + bias_b, NEG)
        m_b = jnp.max(s_b, axis=0, keepdims=True)
        p_b = jnp.exp2(s_b - m_b)
        l_b = jnp.sum(p_b, axis=0, keepdims=True)
        dp_b = nt(kv_prv[h, 1], qdo_nxt[h, 1])
        d_b = jnp.sum(p_b * dp_b, axis=0, keepdims=True)
        pbuf[slot, 2] = p_b
        dpbuf[slot, 2] = dp_b
        sb_own[h, 0:1] = m_b
        sb_own[h, 1:2] = l_b
        sb_own[h, 2:3] = d_b
        sb_own[h, 3:4] = d_b

        @pl.when(has_right)
        def _():
            c_sb(h).start()

    def combine(a, b):
        m_a, m_b = a[0:1], b[0:1]
        m = jnp.maximum(m_a, m_b)
        e_a = jnp.exp2(m_a - m)
        e_b = jnp.exp2(m_b - m)
        inv = 1.0 / (a[1:2] * e_a + b[1:2] * e_b)
        w_a = e_a * inv
        w_b = e_b * inv
        return w_a, w_b, a[2:3] * w_a + b[2:3] * w_b

    def phase2(h):
        slot = lax.rem(h, SLOTS)

        @pl.when(has_left)
        def _():
            c_sb(h).wait_recv()

        @pl.when(has_right)
        def _():
            c_sa(h).wait_recv()

        w_o, _, delta_o = combine(sa_own[h], sb_rcv[h])
        _, w_n, delta_n = combine(sa_nxt[h], sb_own[h])
        k_c, k_p = kv_own[h, 0], kv_prv[h, 0]
        q_o, q_n = qdo_own[h, 0], qdo_nxt[h, 0]
        do_o, do_n = qdo_own[h, 1], qdo_nxt[h, 1]
        p_b = pbuf[slot, 2] * w_n
        ds_b = (p_b * (dpbuf[slot, 2] - delta_n)).astype(BF)
        p_p = pbuf[slot, 1] * w_o
        ds_p = (p_p * (dpbuf[slot, 1] - delta_o)).astype(BF)
        dq_n = (tn(ds_b, k_p) * SCALE).astype(BF)
        dq_snd[h] = dq_n
        dk_p = ((nn(ds_p, q_o) + nn(ds_b, q_n)) * SCALE).astype(BF)
        dv_p = (nn(p_p.astype(BF), do_o) + nn(p_b.astype(BF), do_n)).astype(BF)
        dkv_snd[h, 0] = dk_p
        dkv_snd[h, 1] = dv_p

        p_c = pbuf[slot, 0] * w_o
        ds_c = (p_c * (dpbuf[slot, 0] - delta_o)).astype(BF)
        dk = nn(ds_c, q_o) * SCALE
        dv = nn(p_c.astype(BF), do_o)
        dq = (tn(ds_c, k_c) + tn(ds_p, k_p)) * SCALE
        dkv_loc[h, 0] = dk
        dkv_loc[h, 1] = dv
        dq_loc[h] = dq

    def phase3(h):
        @pl.when(has_left)
        def _():
            c_tx(h).wait_recv()

        @pl.when(has_right)
        def _():
            c_tq(h).wait_recv()

        def own_sums(grad):
            high = grad.astype(BF)
            low = (grad - high.astype(F32)).astype(BF)
            return nn(mem[...], high) + nn(mem[...], low)

        def column_sum(x):
            return jnp.sum(x, axis=0, keepdims=True)

        sums = own_sums(dq_loc[h])
        ssum[h, 0] = sums[:CAP]
        ls_snd[h, 0:1] = sums[CAP : CAP + 1]
        sent = nn(mem_r[...], dq_snd[h])
        from_q[h, 0:1] = sent[CAP : CAP + 1]
        g_acc[0, h] = (
            column_sum(sums[:CAP] * tabq[h].astype(F32))
            + sums[CAP : CAP + 1] * prev_rcv[h]
            + column_sum(sent[:CAP] * tabq_rcv[h].astype(F32))
            + sent[CAP : CAP + 1] * prev_snd[h]
        )
        for part in range(2):
            sums = own_sums(dkv_loc[h, part])
            ssum[h, part + 1] = sums[:CAP]
            ls_snd[h, part + 1 : part + 2] = sums[CAP : CAP + 1]
            sent = nn(mem_l[...], dkv_snd[h, part])
            lp_snd[h, part : part + 1] = sent[CAP : CAP + 1]
            g_acc[0, (part + 1) * HEADS + h] = column_sum(
                sums * tabx[h, part].astype(F32)
            ) + column_sum(sent * tabx_rcv[h, part].astype(F32))
        ls_snd[h, 3:4] = sums[CAP : CAP + 1]

    def out_byte(part, h):
        cb = part * HEADS + h
        return pltpu.make_async_copy(
            out_b.at[h, part], bg_ref.at[0, :, cols(cb)], ob_sem.at[h, part]
        )

    def out_patch(part, h):
        cb = part * HEADS + h
        return pltpu.make_async_copy(
            out_p.at[h, part], pg_ref.at[0, :, cols(cb)], op_sem.at[h, part]
        )

    def send_dkv(h):
        @pl.when(has_left)
        def _():
            c_dkv(h).start()

    def send_dq(h):
        @pl.when(has_right)
        def _():
            c_dq(h).start()

    def send_tables():
        @pl.when(has_left)
        def _():
            for h in range(HEADS):
                c_tq(h).start()

        @pl.when(has_right)
        def _():
            for h in range(HEADS):
                c_tx(h).start()

    def results(h):
        @pl.when(has_left)
        def _():
            c_dq(h).wait_recv()

        @pl.when(has_right)
        def _():
            c_dkv(h).wait_recv()

        for part in range(3):
            if part == 0:
                own, got = dq_loc[h], dq_rcv[h]
            else:
                own, got = dkv_loc[h, part - 1], dkv_rcv[h, part - 1]
            out_b[h, part] = (own + got.astype(F32)).astype(BF)
            out_byte(part, h).start()
            ssum[h, part] += nn(mem[:CAP], got)

    def patch_results(h):
        for part in range(3):
            cb = part * HEADS + h
            after = ls_rcv[h, part : part + 1]
            if part == 0:
                after = after + from_q[h, 0:1]
            total = ssum[h, part] + last_col[...] * after
            out_p[h, part] = (total * gain_ref[:, cols(cb)]).astype(BF)
            out_patch(part, h).start()

    def step(s, carry):
        @pl.when(s < HEADS)
        def _():
            phase1(s)

        @pl.when(s < HEADS - AHEAD)
        def _():
            send_inputs(s + AHEAD)

        @pl.when(s == HEADS - AHEAD)
        def _():
            send_tables()

        @pl.when(s >= LAG2)
        def _():
            phase2(s - LAG2)

        @pl.when(jnp.logical_and(s >= FIRST, s < FIRST + FLIGHT))
        def _():
            send_dkv(s - FIRST)

        @pl.when(s >= FIRST)
        def _():
            send_dq(s - FIRST)

        return carry

    lax.fori_loop(0, HEADS + LAG2, step, 0)

    def gain_copies(t):
        return [
            pltpu.make_async_remote_copy(
                src_ref=g_acc.at[t],
                dst_ref=g_rcv.at[t, k],
                send_sem=gs_sem.at[t, k],
                recv_sem=gr_sem.at[t, k],
                device_id=peer,
                device_id_type=MESH,
            )
            for k, peer in enumerate(groups[t])
        ]

    def gain_start(t):
        for copy in gain_copies(t):
            copy.start()

    def gain_finish(t):
        for copy in gain_copies(t):
            copy.wait_recv()
        total = g_acc[t]
        for k in range(7):
            total = total + g_rcv[t, k]
        if t < 2:
            g_acc[t + 1] = total
        else:
            gg_ref[...] = total / ROWS

    def run_phase3(h, carry):
        phase3(h)
        return carry

    lax.fori_loop(0, HEADS, run_phase3, 0)
    gain_start(0)

    @pl.when(has_left)
    def _():
        c_lp.start()

    for h in range(FLIGHT, HOLD):
        send_dkv(h)
    for h in range(HEADS + LAG2 - FIRST, HEADS):
        send_dq(h)

    def add_lead(h, carry):
        ls_snd[h, 1:3] = ls_snd[h, 1:3] + lp_rcv[h]
        return carry

    def forward_lead():
        @pl.when(has_right)
        def _():
            c_lp.wait_recv()

        lax.fori_loop(0, HEADS, add_lead, 0)

        @pl.when(has_left)
        def _():
            c_ls.start()

    def take_lead():
        @pl.when(has_right)
        def _():
            c_ls.wait_recv()

    for h in range(HEADS):
        results(h)
        if h == 1:
            forward_lead()
            for g in range(HOLD, HEADS):
                send_dkv(g)
        if h == 2:
            gain_finish(0)

            @pl.when(z_hi == 0)
            def _():
                pl.semaphore_wait(hi_sem, 4)

            gain_start(1)
        if h == 4:
            gain_finish(1)
            gain_start(2)
        if h == 6:
            take_lead()
            for g in range(6):
                patch_results(g)
            gain_finish(2)
        if h >= 6:
            patch_results(h)
    for t in range(3):
        for copy in gain_copies(t):
            copy.wait_send()

    def drain(h, carry):
        @pl.when(has_left)
        def _():
            for copy in (c_q(h), c_do(h), c_tq(h), c_sa(h), c_dkv(h)):
                copy.wait_send()

        @pl.when(has_right)
        def _():
            for copy in (c_kv(h), c_tx(h), c_sb(h), c_dq(h)):
                copy.wait_send()

        for part in range(3):
            out_byte(part, h).wait()
            out_patch(part, h).wait()
        return carry

    lax.fori_loop(0, HEADS, drain, 0)

    @pl.when(has_left)
    def _():
        for copy in (c_el, c_lp, c_ls):
            copy.wait_send()

    @pl.when(has_right)
    def _():
        for copy in (c_prev, c_er):
            copy.wait_send()


def local(byte_qkv, patch_qkv, patch_gain, out_grad, patch_slot, lead):
    width = 3 * HEADS * HD
    any_spec = pl.BlockSpec(memory_space=pl.ANY)
    vmem = pl.BlockSpec(memory_space=pltpu.VMEM)
    smem = pl.BlockSpec(memory_space=pltpu.SMEM)
    V = pltpu.VMEM
    byte_grad, patch_grad, gain_grad = pl.pallas_call(
        kernel,
        out_shape=(
            jax.ShapeDtypeStruct((1, ROWS, width), BF),
            jax.ShapeDtypeStruct((1, CAP, width), BF),
            jax.ShapeDtypeStruct((3 * HEADS, 1, HD), F32),
        ),
        in_specs=[any_spec, any_spec, vmem, any_spec, vmem, smem],
        out_specs=(any_spec, any_spec, vmem),
        scratch_shapes=[
            V((ROWS, width), BF),
            V((HEADS, CAP, HD), BF),
            V((HEADS, 2, EXT, HD), BF),
            V((HEADS, CAP, HD), BF),
            V((HEADS, 2, EXT, HD), BF),
            V((ROWS, CAP), BF),
            V((EXT, ROWS), BF),
            V((EXT, ROWS), BF),
            V((EXT, ROWS), BF),
            V((1, ROWS), F32),
            V((1, ROWS), F32),
            V((1, ROWS), F32),
            V((HEADS, 2, ROWS, HD), BF),
            V((HEADS, 2, ROWS, HD), BF),
            V((HEADS, 2, ROWS, HD), BF),
            V((HEADS, 2, ROWS, HD), BF),
            V((HEADS, ROWS, HD), F32),
            V((HEADS, 2, ROWS, HD), F32),
            V((HEADS, ROWS, HD), BF),
            V((HEADS, 2, ROWS, HD), BF),
            V((HEADS, ROWS, HD), BF),
            V((HEADS, 2, ROWS, HD), BF),
            V((SLOTS, 3, ROWS, ROWS), F32),
            V((SLOTS, 3, ROWS, ROWS), F32),
            V((HEADS, 4, ROWS), F32),
            V((HEADS, 4, ROWS), F32),
            V((HEADS, 4, ROWS), F32),
            V((HEADS, 4, ROWS), F32),
            V((3 * HEADS, 1, HD), F32),
            V((3 * HEADS, 1, HD), F32),
            V((HEADS, 2, HD), F32),
            V((HEADS, 2, HD), F32),
            V((HEADS, 4, HD), F32),
            V((HEADS, 4, HD), F32),
            V((HEADS, 1, HD), F32),
            V((CAP, HD), F32),
            V((HEADS, 3, CAP, HD), F32),
            V((HEADS, 3, ROWS, HD), BF),
            V((HEADS, 3, CAP, HD), BF),
            V((3, 3 * HEADS, 1, HD), F32),
            V((3, 7, 3 * HEADS, 1, HD), F32),
            pltpu.SemaphoreType.DMA((1,)),
            pltpu.SemaphoreType.DMA((HEADS,)),
            pltpu.SemaphoreType.DMA((HEADS, 3)),
            pltpu.SemaphoreType.DMA((9, HEADS)),
            pltpu.SemaphoreType.DMA((9, HEADS)),
            pltpu.SemaphoreType.DMA((5,)),
            pltpu.SemaphoreType.DMA((5,)),
            pltpu.SemaphoreType.REGULAR,
            pltpu.SemaphoreType.DMA((HEADS, 3)),
            pltpu.SemaphoreType.DMA((HEADS, 3)),
            pltpu.SemaphoreType.DMA((3, 7)),
            pltpu.SemaphoreType.DMA((3, 7)),
        ],
        compiler_params=pltpu.CompilerParams(
            collective_id=0, has_side_effects=True, vmem_limit_bytes=62 * 2**20
        ),
    )(byte_qkv, patch_qkv, patch_gain.reshape(1, width), out_grad, patch_slot, lead)
    return byte_grad, patch_grad, gain_grad.reshape(width)


def solution(mesh):
    placed = (
        P("dp", "seq", None),
        P("dp", "seq", None),
        P(),
        P("dp", "seq", None),
        P("dp", "seq"),
        P("dp", "seq"),
    )
    return jax.shard_map(
        local,
        mesh=mesh,
        in_specs=placed,
        out_specs=(P("dp", "seq", None), P("dp", "seq", None), P()),
        check_vma=False,
    )
```

```python
import functools
import math

import jax
import jax.numpy as jnp
from jax import lax
from jax.experimental import pallas as pl
from jax.experimental.pallas import tpu as pltpu
from jax.sharding import PartitionSpec as P

HEADS = 8
HD = 128
ROWS = 256
CAP = 64
N_SEQ = 128
MESH = pl.DeviceIdType.MESH
BF = jnp.bfloat16
F32 = jnp.float32

NEG = -1e9
SCALE = 1.0 / math.sqrt(HD)
SCALE2 = SCALE / math.log(2.0)
AHEAD = 3
LAG2 = 3
EXT = 80
SLOTS = LAG2 + 1
SENT = 3
FIRST = 7

K_Q, K_DO, K_KV, K_SA, K_SB, K_DKV, K_DQ, K_TQ, K_TX = range(9)
O_PREV, O_EL, O_ER, O_LP, O_LS, O_P2 = range(6)


def nt(a, b):
    return lax.dot_general(a, b, (((1,), (1,)), ((), ())), preferred_element_type=F32)


def nn(a, b):
    return lax.dot_general(a, b, (((1,), (0,)), ((), ())), preferred_element_type=F32)


def tn(a, b):
    return lax.dot_general(a, b, (((0,), (0,)), ((), ())), preferred_element_type=F32)


def cols(block):
    return pl.ds(pl.multiple_of(block * HD, HD), HD)


def peer_groups(me, dp):
    y = lax.rem(me, 8)
    x = lax.rem(me // 8, 4)
    z_lo = me // 32
    z_hi = dp // 2
    core = lax.rem(dp, 2)
    along_z, along_xc, along_y = [], [], []
    for k in range(1, 8):
        z = lax.rem(z_hi * 4 + z_lo + k, 8)
        along_z.append(((lax.rem(z, 4) * 4 + x) * 8 + y, (z // 4) * 2 + core))
        p = lax.rem(x * 2 + core + k, 8)
        along_xc.append(((z_lo * 4 + p // 2) * 8 + y, z_hi * 2 + lax.rem(p, 2)))
        along_y.append(((z_lo * 4 + x) * 8 + lax.rem(y + k, 8), dp))
    return along_y, along_z, along_xc


def kernel(
    byte_ref,
    patch_ref,
    gain_ref,
    cot_ref,
    slot_ref,
    lead_ref,
    bg_ref,
    pg_ref,
    gg_ref,
    byte_v,
    tabq,
    tabx,
    tabq_rcv,
    tabx_rcv,
    oh,
    mem,
    mem_l,
    mem_r,
    effs,
    effs_l,
    effs_r,
    qdo_own,
    kv_own,
    qdo_nxt,
    kv_prv,
    dq_loc,
    dkv_loc,
    dq_snd,
    dkv_snd,
    dq_rcv,
    dkv_rcv,
    pbuf,
    dpbuf,
    sa_own,
    sa_nxt,
    sb_own,
    sb_rcv,
    prev_snd,
    prev_rcv,
    prev2_rcv,
    lp_snd,
    lp_rcv,
    ls_snd,
    ls_rcv,
    from_q,
    last_col,
    ssum,
    out_b,
    out_p,
    g_acc,
    g_part,
    g_rcv,
    g_all,
    in_sem,
    do_sem,
    tab_sem,
    s_sem,
    r_sem,
    one_s,
    one_r,
    hi_sem,
    ob_sem,
    op_sem,
    gs_sem,
    gr_sem,
):
    me = lax.axis_index("seq")
    dp = lax.axis_index("dp")
    has_left = me > 0
    has_right = me < N_SEQ - 1
    left = (me - 1, dp)
    right = (me + 1, dp)
    groups = peer_groups(me, dp)

    barrier = pltpu.get_barrier_semaphore()

    @pl.when(has_left)
    def _():
        pl.semaphore_signal(barrier, inc=1, device_id=left, device_id_type=MESH)

    @pl.when(has_right)
    def _():
        pl.semaphore_signal(barrier, inc=1, device_id=right, device_id_type=MESH)

    x = lax.rem(me // 8, 4)
    y = lax.rem(me, 8)
    z = (dp // 2) * 4 + me // 32
    core = lax.rem(dp, 2)

    def greet(sem, peer):
        pl.semaphore_signal(sem, inc=1, device_id=peer, device_id_type=MESH)

    def at(x_, z_, core_):
        return (((z_ % 4) * 4 + x_) * 8 + y, (z_ // 4) * 2 + core_)

    for peer in groups[0]:
        greet(barrier, peer)
    greet(barrier, (me, dp + 1 - 2 * core))
    for k in range(8):

        @pl.when(k > z)
        def _():
            greet(barrier, at(x, k, core))

    for k in range(4):

        @pl.when(k > x)
        def _():
            greet(barrier, (me + (k - x) * 8, dp))
            greet(barrier, (me + (k - x) * 8, dp + 1 - 2 * core))

    def load_tables(h):
        return [
            pltpu.make_async_copy(
                patch_ref.at[0, :, cols(h)], tabq.at[h], tab_sem.at[h, 0]
            )
        ] + [
            pltpu.make_async_copy(
                patch_ref.at[0, :, cols((part + 1) * HEADS + h)],
                tabx.at[h, part],
                tab_sem.at[h, part + 1],
            )
            for part in range(2)
        ]

    for h in range(HEADS):
        for load in load_tables(h):
            load.start()
    load_byte = pltpu.make_async_copy(byte_ref.at[0], byte_v, in_sem.at[0])
    load_byte.start()

    def load_do(h):
        return pltpu.make_async_copy(cot_ref.at[0, :, cols(h)], qdo_own.at[h, 1], do_sem.at[h])

    for h in range(HEADS):
        load_do(h).start()

    lead = lead_ref[0, 0]
    slots = slot_ref[...]
    lane_i = lax.broadcasted_iota(jnp.int32, (1, ROWS), 1)
    effs[...] = jnp.where(lane_i < lead, CAP, slots).astype(F32)

    def members(eff):
        row_i = lax.broadcasted_iota(jnp.int32, (EXT, ROWS), 0).astype(F32)
        return jnp.where(row_i == eff, 1.0, 0.0).astype(BF)

    mem[...] = members(effs[...])
    slot_i = lax.broadcasted_iota(jnp.int32, (HD, ROWS), 0)
    pick = jnp.where(slot_i == slots, 1.0, 0.0)
    oh[...] = jnp.transpose(pick)[:, :CAP].astype(BF)
    last_col[...] = jnp.broadcast_to(pick[:CAP, ROWS - 1 : ROWS], (CAP, HD))

    @pl.when(jnp.logical_not(has_left))
    def _():
        kv_prv[...] = jnp.zeros_like(kv_prv)
        tabx_rcv[...] = jnp.zeros_like(tabx_rcv)
        effs_l[...] = jnp.zeros_like(effs_l)
        dq_rcv[...] = jnp.zeros_like(dq_rcv)
        prev_rcv[...] = jnp.zeros_like(prev_rcv)
        prev2_rcv[...] = jnp.zeros_like(prev2_rcv)
        sb_rcv[...] = jnp.full(sb_rcv.shape, NEG, F32)

    @pl.when(jnp.logical_not(has_right))
    def _():
        qdo_nxt[...] = jnp.zeros_like(qdo_nxt)
        dkv_rcv[...] = jnp.zeros_like(dkv_rcv)
        ls_rcv[...] = jnp.zeros_like(ls_rcv)
        lp_rcv[...] = jnp.zeros_like(lp_rcv)
        tabq_rcv[...] = jnp.zeros_like(tabq_rcv)
        effs_r[...] = jnp.zeros_like(effs_r)
        sa_nxt[...] = jnp.ones_like(sa_nxt)

    for h in range(HEADS):
        for load in load_tables(h):
            load.wait()
    load_byte.wait()

    def hidden_dst(part, h):
        return qdo_own.at[h, 0] if part == 0 else kv_own.at[h, part - 1]

    def make_hidden(h, carry):
        for part in range(3):
            cb = part * HEADS + h
            rows = nn(oh[...], tabq[h] if part == 0 else tabx[h, part - 1])
            prev_snd[cb] = rows[ROWS - 1 : ROWS]
            hidden = gain_ref[:, cols(cb)] * rows + byte_v[:, cols(cb)].astype(F32)
            hidden_dst(part, h)[...] = hidden.astype(BF)
        return carry

    lax.fori_loop(0, HEADS, make_hidden, 0)
    for h in range(HEADS):
        load_do(h).wait()

    neighbours = has_left.astype(jnp.int32) + has_right.astype(jnp.int32)
    pl.semaphore_wait(barrier, neighbours + 8 + z + 2 * x)

    def answer():
        for k in range(8):

            @pl.when(k < z)
            def _():
                greet(hi_sem, at(x, k, core))

        for k in range(4):

            @pl.when(k < x)
            def _():
                greet(hi_sem, (me + (k - x) * 8, dp))
                greet(hi_sem, (me + (k - x) * 8, dp + 1 - 2 * core))

    def remote(kind, h, src, dst, to):
        return pltpu.make_async_remote_copy(
            src_ref=src,
            dst_ref=dst,
            send_sem=s_sem.at[kind, h],
            recv_sem=r_sem.at[kind, h],
            device_id=to,
            device_id_type=MESH,
        )

    def c_q(h):
        return remote(K_Q, h, qdo_own.at[h, 0], qdo_nxt.at[h, 0], left)

    def c_do(h):
        return remote(K_DO, h, qdo_own.at[h, 1], qdo_nxt.at[h, 1], left)

    def c_kv(h):
        return remote(K_KV, h, kv_own.at[h], kv_prv.at[h], right)

    def c_sa(h):
        return remote(K_SA, h, sa_own.at[h], sa_nxt.at[h], left)

    def c_sb(h):
        return remote(K_SB, h, sb_own.at[h], sb_rcv.at[h], right)

    def c_dkv(h):
        return remote(K_DKV, h, dkv_snd.at[h], dkv_rcv.at[h], left)

    def c_dq(h):
        return remote(K_DQ, h, dq_snd.at[h], dq_rcv.at[h], right)

    def c_tq(h):
        return remote(K_TQ, h, tabq.at[h], tabq_rcv.at[h], left)

    def c_tx(h):
        return remote(K_TX, h, tabx.at[h], tabx_rcv.at[h], right)

    def once(kind, src, dst, to):
        return pltpu.make_async_remote_copy(
            src_ref=src,
            dst_ref=dst,
            send_sem=one_s.at[kind],
            recv_sem=one_r.at[kind],
            device_id=to,
            device_id_type=MESH,
        )

    c_prev = once(O_PREV, prev_snd, prev_rcv, right)
    c_el = once(O_EL, effs, effs_r, left)
    c_er = once(O_ER, effs, effs_l, right)
    c_p2 = once(O_P2, prev_rcv, prev2_rcv, right)
    c_lp = once(O_LP, lp_snd, lp_rcv, left)
    c_ls = once(O_LS, ls_snd, ls_rcv, left)

    @pl.when(has_right)
    def _():
        c_prev.start()
        c_er.start()

    @pl.when(has_left)
    def _():
        c_el.start()
        for h in range(AHEAD):
            c_do(h).start()
        c_prev.wait_recv()

    lead_rows = lax.broadcasted_iota(jnp.int32, (16, HD), 0) < lead

    def fix_hidden(h, carry):
        for part in range(3):
            cb = part * HEADS + h
            dst = hidden_dst(part, h)
            fixed = gain_ref[:, cols(cb)] * prev_rcv[cb] + byte_v[:16, cols(cb)].astype(F32)
            dst[:16] = jnp.where(lead_rows, fixed, dst[:16].astype(F32)).astype(BF)
        return carry

    lax.fori_loop(0, HEADS, fix_hidden, 0)

    def send_inputs(h, with_do=True):
        @pl.when(has_left)
        def _():
            c_q(h).start()
            if with_do:
                c_do(h).start()

        @pl.when(has_right)
        def _():
            c_kv(h).start()

    for h in range(AHEAD):
        send_inputs(h, False)
    answer()

    @pl.when(has_right)
    def _():
        c_p2.start()

    @pl.when(has_left)
    def _():
        c_er.wait_recv()
        c_p2.wait_recv()

    @pl.when(has_right)
    def _():
        c_el.wait_recv()

    mem_l[...] = members(effs_l[...])
    mem_r[...] = members(effs_r[...])

    def phase1(h):
        slot = lax.rem(h, SLOTS)

        @pl.when(has_left)
        def _():
            c_kv(h).wait_recv()

        @pl.when(has_right)
        def _():
            c_q(h).wait_recv()
            c_do(h).wait_recv()

        key_i = lax.broadcasted_iota(jnp.int32, (ROWS, ROWS), 0)
        query_i = lax.broadcasted_iota(jnp.int32, (ROWS, ROWS), 1)
        bias_p = jnp.where(has_left, 0.0, NEG)
        bias_b = jnp.where(jnp.logical_and(has_left, has_right), 0.0, NEG)
        k_c, k_p = kv_own[h, 0], kv_prv[h, 0]
        q_o, q_n = qdo_own[h, 0], qdo_nxt[h, 0]
        s_c = jnp.where(key_i <= query_i, nt(k_c, q_o) * SCALE2, NEG)
        s_p = nt(k_p, q_o) * SCALE2 + bias_p
        m_a = jnp.maximum(
            jnp.max(s_c, axis=0, keepdims=True), jnp.max(s_p, axis=0, keepdims=True)
        )
        p_c = jnp.exp2(s_c - m_a)
        p_p = jnp.exp2(s_p - m_a)
        l_a = jnp.sum(p_c, axis=0, keepdims=True) + jnp.sum(p_p, axis=0, keepdims=True)
        dp_c = nt(kv_own[h, 1], qdo_own[h, 1])
        dp_p = nt(kv_prv[h, 1], qdo_own[h, 1])
        d_a = jnp.sum(p_c * dp_c, axis=0, keepdims=True) + jnp.sum(
            p_p * dp_p, axis=0, keepdims=True
        )
        pbuf[slot, 0] = p_c
        pbuf[slot, 1] = p_p
        dpbuf[slot, 0] = dp_c
        dpbuf[slot, 1] = dp_p
        sa_own[h, 0:1] = m_a
        sa_own[h, 1:2] = l_a
        sa_own[h, 2:3] = d_a
        sa_own[h, 3:4] = d_a

        @pl.when(has_left)
        def _():
            c_sa(h).start()

        s_b = jnp.where(key_i > query_i, nt(k_p, q_n) * SCALE2 + bias_b, NEG)
        m_b = jnp.max(s_b, axis=0, keepdims=True)
        p_b = jnp.exp2(s_b - m_b)
        l_b = jnp.sum(p_b, axis=0, keepdims=True)
        dp_b = nt(kv_prv[h, 1], qdo_nxt[h, 1])
        d_b = jnp.sum(p_b * dp_b, axis=0, keepdims=True)
        pbuf[slot, 2] = p_b
        dpbuf[slot, 2] = dp_b
        sb_own[h, 0:1] = m_b
        sb_own[h, 1:2] = l_b
        sb_own[h, 2:3] = d_b
        sb_own[h, 3:4] = d_b

        @pl.when(has_right)
        def _():
            c_sb(h).start()

    def combine(a, b):
        m_a, m_b = a[0:1], b[0:1]
        m = jnp.maximum(m_a, m_b)
        e_a = jnp.exp2(m_a - m)
        e_b = jnp.exp2(m_b - m)
        inv = 1.0 / (a[1:2] * e_a + b[1:2] * e_b)
        w_a = e_a * inv
        w_b = e_b * inv
        return w_a, w_b, a[2:3] * w_a + b[2:3] * w_b

    def phase2(h):
        slot = lax.rem(h, SLOTS)

        @pl.when(has_left)
        def _():
            c_sb(h).wait_recv()

        @pl.when(has_right)
        def _():
            c_sa(h).wait_recv()

        w_o, _, delta_o = combine(sa_own[h], sb_rcv[h])
        _, w_n, delta_n = combine(sa_nxt[h], sb_own[h])
        k_c, k_p = kv_own[h, 0], kv_prv[h, 0]
        q_o, q_n = qdo_own[h, 0], qdo_nxt[h, 0]
        do_o, do_n = qdo_own[h, 1], qdo_nxt[h, 1]
        p_b = pbuf[slot, 2] * w_n
        ds_b = (p_b * (dpbuf[slot, 2] - delta_n)).astype(BF)
        p_p = pbuf[slot, 1] * w_o
        ds_p = (p_p * (dpbuf[slot, 1] - delta_o)).astype(BF)
        dq_n = (tn(ds_b, k_p) * SCALE).astype(BF)
        dq_snd[h] = dq_n
        dk_p = ((nn(ds_p, q_o) + nn(ds_b, q_n)) * SCALE).astype(BF)
        dv_p = (nn(p_p.astype(BF), do_o) + nn(p_b.astype(BF), do_n)).astype(BF)
        dkv_snd[h, 0] = dk_p
        dkv_snd[h, 1] = dv_p

        p_c = pbuf[slot, 0] * w_o
        ds_c = (p_c * (dpbuf[slot, 0] - delta_o)).astype(BF)
        dk = nn(ds_c, q_o) * SCALE
        dv = nn(p_c.astype(BF), do_o)
        dq = (tn(ds_c, k_c) + tn(ds_p, k_p)) * SCALE
        dkv_loc[h, 0] = dk
        dkv_loc[h, 1] = dv
        dq_loc[h] = dq

    def phase3(h):
        @pl.when(has_left)
        def _():
            c_tx(h).wait_recv()

        @pl.when(has_right)
        def _():
            c_tq(h).wait_recv()

        def own_sums(grad):
            high = grad.astype(BF)
            low = (grad - high.astype(F32)).astype(BF)
            return nn(mem[...], high) + nn(mem[...], low)

        def column_sum(x):
            return jnp.sum(x, axis=0, keepdims=True)

        sums = own_sums(dq_loc[h])
        ssum[h, 0] = sums[:CAP]
        ls_snd[h, 0:1] = sums[CAP : CAP + 1]
        sent = nn(mem_r[...], dq_snd[h])
        from_q[h, 0:1] = sent[CAP : CAP + 1]
        g_acc[h] = (
            column_sum(sums[:CAP] * tabq[h].astype(F32))
            + sums[CAP : CAP + 1] * prev_rcv[h]
            + column_sum(sent[:CAP] * tabq_rcv[h].astype(F32))
            + sent[CAP : CAP + 1] * prev_snd[h]
        )
        for part in range(2):
            sums = own_sums(dkv_loc[h, part])
            ssum[h, part + 1] = sums[:CAP]
            ls_snd[h, part + 1 : part + 2] = sums[CAP : CAP + 1]
            sent = nn(mem_l[...], dkv_snd[h, part])
            lp_snd[h, part : part + 1] = sent[CAP : CAP + 1]
            cb = (part + 1) * HEADS + h
            g_acc[cb] = (
                column_sum(sums[:CAP] * tabx[h, part].astype(F32))
                + sums[CAP : CAP + 1] * prev_rcv[cb]
                + column_sum(sent[:CAP] * tabx_rcv[h, part].astype(F32))
                + sent[CAP : CAP + 1] * prev2_rcv[cb]
            )
        ls_snd[h, 3:4] = sums[CAP : CAP + 1]

    def out_byte(part, h):
        cb = part * HEADS + h
        return pltpu.make_async_copy(
            out_b.at[h, part], bg_ref.at[0, :, cols(cb)], ob_sem.at[h, part]
        )

    def out_patch(part, h):
        cb = part * HEADS + h
        return pltpu.make_async_copy(
            out_p.at[h, part], pg_ref.at[0, :, cols(cb)], op_sem.at[h, part]
        )

    def send_dkv(h):
        @pl.when(has_left)
        def _():
            c_dkv(h).start()

    def send_dq(h):
        @pl.when(has_right)
        def _():
            c_dq(h).start()

    def send_tables():
        @pl.when(has_left)
        def _():
            for h in range(HEADS):
                c_tq(h).start()

        @pl.when(has_right)
        def _():
            for h in range(HEADS):
                c_tx(h).start()

    def results(h):
        @pl.when(has_left)
        def _():
            c_dq(h).wait_recv()

        @pl.when(has_right)
        def _():
            c_dkv(h).wait_recv()

        for part in range(3):
            if part == 0:
                own, got = dq_loc[h], dq_rcv[h]
            else:
                own, got = dkv_loc[h, part - 1], dkv_rcv[h, part - 1]
            out_b[h, part] = (own + got.astype(F32)).astype(BF)
            out_byte(part, h).start()
            ssum[h, part] += nn(mem[:CAP], got)

    def patch_results(h):
        for part in range(3):
            cb = part * HEADS + h
            after = ls_rcv[h, part : part + 1]
            if part == 0:
                after = after + from_q[h, 0:1]
            total = ssum[h, part] + last_col[...] * after
            out_p[h, part] = (total * gain_ref[:, cols(cb)]).astype(BF)
            out_patch(part, h).start()

    def step(s, carry):
        @pl.when(s < HEADS)
        def _():
            phase1(s)

        @pl.when(s < HEADS - AHEAD)
        def _():
            send_inputs(s + AHEAD)

        @pl.when(s == HEADS - AHEAD)
        def _():
            send_tables()

        @pl.when(s >= LAG2)
        def _():
            phase2(s - LAG2)

        @pl.when(jnp.logical_and(s >= FIRST, s < FIRST + SENT))
        def _():
            send_dkv(s - FIRST)

        @pl.when(s >= FIRST)
        def _():
            send_dq(s - FIRST)

        return carry

    lax.fori_loop(0, HEADS + LAG2, step, 0)

    pos = x * 2 + core
    stages = (groups[2], groups[0], groups[1], groups[2])

    def share(p):
        return pl.ds(p * 3, 3)

    def gain_copies(t):
        copies = []
        for k, peer in enumerate(stages[t]):
            if t == 0:
                src, dst = g_acc.at[share(lax.rem(pos + k + 1, 8))], g_rcv.at[0, k]
            elif t < 3:
                src, dst = g_part.at[t - 1], g_rcv.at[t, k]
            else:
                src, dst = g_all.at[share(pos)], g_all.at[share(pos)]
            copies.append(
                pltpu.make_async_remote_copy(
                    src_ref=src,
                    dst_ref=dst,
                    send_sem=gs_sem.at[t, k],
                    recv_sem=gr_sem.at[t, k],
                    device_id=peer,
                    device_id_type=MESH,
                )
            )
        return copies

    def gain_start(t):
        for copy in gain_copies(t):
            copy.start()

    def gain_finish(t):
        for copy in gain_copies(t):
            copy.wait_recv()
        if t == 3:
            gg_ref[...] = g_all[...] / ROWS
            return
        total = g_acc[share(pos)] if t == 0 else g_part[t - 1]
        for k in range(7):
            total = total + g_rcv[t, k]
        if t < 2:
            g_part[t] = total
        else:
            g_all[share(pos)] = total

    def run_phase3(h, carry):
        phase3(h)
        return carry

    lax.fori_loop(0, HEADS, run_phase3, 0)
    answers = 7 - z + 2 * (3 - x)

    @pl.when(answers > 0)
    def _():
        pl.semaphore_wait(hi_sem, answers)

    gain_start(0)

    @pl.when(has_left)
    def _():
        c_lp.start()

    send_dkv(SENT)
    for h in range(HEADS + LAG2 - FIRST, HEADS):
        send_dq(h)

    def add_lead(h, carry):
        ls_snd[h, 1:3] = ls_snd[h, 1:3] + lp_rcv[h]
        return carry

    def forward_lead():
        @pl.when(has_right)
        def _():
            c_lp.wait_recv()

        lax.fori_loop(0, HEADS, add_lead, 0)

        @pl.when(has_left)
        def _():
            c_ls.start()

    def take_lead():
        @pl.when(has_right)
        def _():
            c_ls.wait_recv()

    for h in range(HEADS):
        results(h)
        if h == 0:
            gain_finish(0)
            gain_start(1)
            for g in range(SENT + 1, 6):
                send_dkv(g)
        if h == 1:
            forward_lead()
            for g in range(6, HEADS):
                send_dkv(g)
        if h == 3:
            gain_finish(1)
            gain_start(2)
        if h == 5:
            gain_finish(2)
            gain_start(3)
            take_lead()
            for g in range(5):
                patch_results(g)
        if h >= 5:
            patch_results(h)
    gain_finish(3)
    for t in range(4):
        for copy in gain_copies(t):
            copy.wait_send()

    def drain(h, carry):
        @pl.when(has_left)
        def _():
            for copy in (c_q(h), c_do(h), c_tq(h), c_sa(h), c_dkv(h)):
                copy.wait_send()

        @pl.when(has_right)
        def _():
            for copy in (c_kv(h), c_tx(h), c_sb(h), c_dq(h)):
                copy.wait_send()

        for part in range(3):
            out_byte(part, h).wait()
            out_patch(part, h).wait()
        return carry

    lax.fori_loop(0, HEADS, drain, 0)

    @pl.when(has_left)
    def _():
        for copy in (c_el, c_lp, c_ls):
            copy.wait_send()

    @pl.when(has_right)
    def _():
        for copy in (c_prev, c_er, c_p2):
            copy.wait_send()


CHUNKS = 8


def place(byte_in, patch_in, gain_in, byte_out, patch_out, gain_out, byte_v, patch_v, gain_v, sem):
    rows = ROWS // CHUNKS
    moves = [
        (
            byte_in.at[0, pl.ds(k * rows, rows)],
            byte_v.at[pl.ds(k * rows, rows)],
            byte_out.at[0, pl.ds(k * rows, rows)],
        )
        for k in range(CHUNKS)
    ] + [(patch_in, patch_v, patch_out), (gain_in, gain_v, gain_out)]
    loads = [
        pltpu.make_async_copy(src, mid, sem.at[0, k]) for k, (src, mid, _) in enumerate(moves)
    ]
    stores = [
        pltpu.make_async_copy(mid, dst, sem.at[1, k]) for k, (_, mid, dst) in enumerate(moves)
    ]
    for load in loads:
        load.start()
    for load, store in zip(loads, stores):
        load.wait()
        store.start()
    for store in stores:
        store.wait()


def local(byte_qkv, patch_qkv, patch_gain, out_grad, patch_slot, lead):
    width = 3 * HEADS * HD
    any_spec = pl.BlockSpec(memory_space=pl.ANY)
    vmem = pl.BlockSpec(memory_space=pltpu.VMEM)
    smem = pl.BlockSpec(memory_space=pltpu.SMEM)
    V = pltpu.VMEM
    byte_grad, patch_grad, gain_grad = pl.pallas_call(
        kernel,
        out_shape=(
            jax.ShapeDtypeStruct((1, ROWS, width), BF),
            jax.ShapeDtypeStruct((1, CAP, width), BF),
            jax.ShapeDtypeStruct((3 * HEADS, 1, HD), F32),
        ),
        in_specs=[any_spec, any_spec, vmem, any_spec, vmem, smem],
        out_specs=(any_spec, any_spec, vmem),
        scratch_shapes=[
            V((ROWS, width), BF),
            V((HEADS, CAP, HD), BF),
            V((HEADS, 2, CAP, HD), BF),
            V((HEADS, CAP, HD), BF),
            V((HEADS, 2, CAP, HD), BF),
            V((ROWS, CAP), BF),
            V((EXT, ROWS), BF),
            V((EXT, ROWS), BF),
            V((EXT, ROWS), BF),
            V((1, ROWS), F32),
            V((1, ROWS), F32),
            V((1, ROWS), F32),
            V((HEADS, 2, ROWS, HD), BF),
            V((HEADS, 2, ROWS, HD), BF),
            V((HEADS, 2, ROWS, HD), BF),
            V((HEADS, 2, ROWS, HD), BF),
            V((HEADS, ROWS, HD), F32),
            V((HEADS, 2, ROWS, HD), F32),
            V((HEADS, ROWS, HD), BF),
            V((HEADS, 2, ROWS, HD), BF),
            V((HEADS, ROWS, HD), BF),
            V((HEADS, 2, ROWS, HD), BF),
            V((SLOTS, 3, ROWS, ROWS), F32),
            V((SLOTS, 3, ROWS, ROWS), F32),
            V((HEADS, 4, ROWS), F32),
            V((HEADS, 4, ROWS), F32),
            V((HEADS, 4, ROWS), F32),
            V((HEADS, 4, ROWS), F32),
            V((3 * HEADS, 1, HD), F32),
            V((3 * HEADS, 1, HD), F32),
            V((3 * HEADS, 1, HD), F32),
            V((HEADS, 2, HD), F32),
            V((HEADS, 2, HD), F32),
            V((HEADS, 4, HD), F32),
            V((HEADS, 4, HD), F32),
            V((HEADS, 1, HD), F32),
            V((CAP, HD), F32),
            V((HEADS, 3, CAP, HD), F32),
            V((HEADS, 3, ROWS, HD), BF),
            V((HEADS, 3, CAP, HD), BF),
            V((3 * HEADS, 1, HD), F32),
            V((2, 3, 1, HD), F32),
            V((3, 7, 3, 1, HD), F32),
            V((3 * HEADS, 1, HD), F32),
            pltpu.SemaphoreType.DMA((1,)),
            pltpu.SemaphoreType.DMA((HEADS,)),
            pltpu.SemaphoreType.DMA((HEADS, 3)),
            pltpu.SemaphoreType.DMA((9, HEADS)),
            pltpu.SemaphoreType.DMA((9, HEADS)),
            pltpu.SemaphoreType.DMA((6,)),
            pltpu.SemaphoreType.DMA((6,)),
            pltpu.SemaphoreType.REGULAR,
            pltpu.SemaphoreType.DMA((HEADS, 3)),
            pltpu.SemaphoreType.DMA((HEADS, 3)),
            pltpu.SemaphoreType.DMA((4, 7)),
            pltpu.SemaphoreType.DMA((4, 7)),
        ],
        compiler_params=pltpu.CompilerParams(
            collective_id=0, has_side_effects=True, vmem_limit_bytes=62 * 2**20
        ),
    )(byte_qkv, patch_qkv, patch_gain.reshape(1, width), out_grad, patch_slot, lead)
    byte_grad, patch_grad, gain_grad = pl.pallas_call(
        place,
        out_shape=(
            jax.ShapeDtypeStruct((1, ROWS, width), BF),
            jax.ShapeDtypeStruct((1, CAP, width), BF),
            jax.ShapeDtypeStruct((3 * HEADS, 1, HD), F32),
        ),
        in_specs=[any_spec] * 3,
        out_specs=(any_spec,) * 3,
        scratch_shapes=[
            V((ROWS, width), BF),
            V((1, CAP, width), BF),
            V((3 * HEADS, 1, HD), F32),
            pltpu.SemaphoreType.DMA((2, CHUNKS + 2)),
        ],
        compiler_params=pltpu.CompilerParams(vmem_limit_bytes=62 * 2**20),
    )(byte_grad, patch_grad, gain_grad)
    return byte_grad, patch_grad, gain_grad.reshape(width)


def solution(mesh):
    placed = (
        P("dp", "seq", None),
        P("dp", "seq", None),
        P(),
        P("dp", "seq", None),
        P("dp", "seq"),
        P("dp", "seq"),
    )
    return jax.shard_map(
        local,
        mesh=mesh,
        in_specs=placed,
        out_specs=(P("dp", "seq", None), P("dp", "seq", None), P()),
        check_vma=False,
    )
```
